32 devices in a mesh: chan: 8 (over y, x, core), win: 4 (over z).
Axes of the slice: x: 2, y: 2, z: 4, core: 2. Of those that a mesh axis runs over, the one named last changes fastest.
Arguments:
- spectra: float32 [4, 256, 2, 4096], P('win', 'chan'), may hold values from -2000 to 2000
- sources: int32 [2, 8], replicated, may hold values from 0 to 255, as said below
- window_valid: int32 [4, 256], P('win', 'chan'), may hold values 0 or 1
Outputs:
- correlations: float32 [2, 8, 256, 256], P(None, 'win', 'chan')
The draws below stay inside these ranges and needn't reach their ends.
Inputs may be any that keep to these rules, and one draw needn't show every extreme that they name: sources[t, s] is a channel of owner s, that is between (s) * 32 and (s + 1) * 32 - 1; the entries of one turn are distinct.
All inputs are finite; a program needn't handle non-finite values. No bound on the sum of `window_valid` on one device may be relied on, other than what follows from the above.
Results may differ from the reference program's by a relative error of at most 0.0022.
Values may be sent and summed in bfloat16 or wider, within the bound.
A program may use at most 64 MiB of HBM per device.

```python
import math
import jax
import jax.numpy as jnp
from jax import lax

F = 4096
LAGS = 256
CH_DEV = 32
SRC_OWN = 1
TURNS = 2
C = 256
W = 4
SRC = 8


def draw_spectra(key, part):
    key_list = jax.random.split(key, 5)
    base_noise = jnp.clip(jax.random.normal(key_list[0], (W, C, 2, F), jnp.float32), -5.0, 5.0)
    row_spread = jnp.log(10.0)
    col_spread = jnp.log(10.0)
    common_wave = jnp.clip(jax.random.normal(key_list[3], (W, 1, 2, F), jnp.float32), -5.0, 5.0)
    chan_ids = jnp.arange(C, dtype=jnp.int32)
    moveout = chan_ids * (LAGS // 2) // C - LAGS // 4
    jitter = jax.random.randint(key_list[4], (C,), -(LAGS // 8), LAGS // 8 + 1, dtype=jnp.int32)
    delays = moveout + jitter
    freq_bins = jnp.arange(F, dtype=jnp.int32)
    phase_index = delays[:, None] * freq_bins[None, :] % (2 * F)
    angles = phase_index.astype(jnp.float32) * (jnp.pi / F)
    cos_part = jnp.cos(angles)[None, :, :]
    sin_part = jnp.sin(angles)[None, :, :]
    common_real = common_wave[:, :, 0, :] * cos_part + common_wave[:, :, 1, :] * sin_part
    common_imag = common_wave[:, :, 1, :] * cos_part - common_wave[:, :, 0, :] * sin_part
    delayed_wave = jnp.stack([common_real, common_imag], axis=2)
    base_noise = base_noise + 0.8 * delayed_wave
    row_scale = jnp.exp(jax.random.uniform(key_list[1], (W, C, 1, 1), jnp.float32) * row_spread)
    col_scale = jnp.exp(jax.random.uniform(key_list[2], (1, 1, 1, F), jnp.float32) * col_spread)
    return base_noise * row_scale * col_scale


def draw_sources(key, part):
    owners = SRC // SRC_OWN
    key_list = jax.random.split(key, TURNS * owners)
    chosen = jax.vmap(lambda single_key: jax.random.permutation(single_key, CH_DEV)[:SRC_OWN])(key_list)
    offsets = (jnp.arange(owners, dtype=jnp.int32) * CH_DEV)[None, :, None]
    return (chosen.reshape(TURNS, owners, SRC_OWN).astype(jnp.int32) + offsets).reshape(TURNS, SRC)


def set_ends(values, stream_key, low, high):
    place = [jax.random.randint(jax.random.fold_in(stream_key, axis), (), 0, length) for axis, length in enumerate(values.shape)]
    longest = values.shape.index(max(values.shape))
    next_to = place[:longest] + [(place[longest] + 1) % values.shape[longest]] + place[longest + 1:]
    return values.at[tuple(place)].set(low).at[tuple(next_to)].set(high)


def setup_inputs(seed: int = 0) -> dict:
    streams_of = jax.random.split(jax.random.key(seed), 4)
    return {
        "spectra": draw_spectra(jax.random.fold_in(streams_of[3], 71), 0),
        "sources": draw_sources(jax.random.fold_in(streams_of[3], 71), 0),
        "window_valid": set_ends((jax.random.randint(streams_of[2], (W, C), 0, 8) < 7).astype(jnp.int32), jax.random.fold_in(streams_of[2], 1), 0, 1),
    }


def whiten(spectra, window_valid):
    mean_power = lax.optimization_barrier(jnp.mean(spectra * spectra, axis=(2, 3), keepdims=True))
    valid_flags = window_valid.astype(jnp.float32)[:, :, None, None]
    whitened = valid_flags * spectra / jnp.sqrt(mean_power + 1e-05)
    return whitened.astype(jnp.bfloat16).reshape(spectra.shape[0], spectra.shape[1], 2 * spectra.shape[3])

def build_table(freq_count, lag_count):
    shifts = jnp.arange(lag_count, dtype=jnp.int32) - lag_count // 2
    freq_bins = jnp.arange(freq_count, dtype=jnp.int32)
    phase_index = freq_bins[:, None] * shifts[None, :] % (2 * freq_count)
    angles = phase_index.astype(jnp.float32) * (math.pi / freq_count)
    return jnp.concatenate([jnp.cos(angles), -jnp.sin(angles)], axis=0).astype(jnp.bfloat16)

def cross_block(source_piece, receivers, trig_table):
    half_width = receivers.shape[2] // 2
    src_real = source_piece[:, :, None, :half_width].astype(jnp.float32)
    src_imag = source_piece[:, :, None, half_width:].astype(jnp.float32)
    rec_real = receivers[:, None, :, :half_width].astype(jnp.float32)
    rec_imag = receivers[:, None, :, half_width:].astype(jnp.float32)
    cross_real = (src_real * rec_real + src_imag * rec_imag).astype(jnp.bfloat16)
    cross_imag = (src_imag * rec_real - src_real * rec_imag).astype(jnp.bfloat16)
    cross_both = jnp.concatenate([cross_real, cross_imag], axis=-1)
    lag_values = jnp.dot(cross_both.reshape(-1, 2 * half_width).astype(jnp.float32), trig_table.astype(jnp.float32), preferred_element_type=jnp.float32)
    lag_values = lag_values.reshape(source_piece.shape[0], source_piece.shape[1], receivers.shape[1], -1)
    return lax.optimization_barrier(jnp.sum(lag_values, axis=0))

def reference(spectra, sources, window_valid):
    whitened = whiten(spectra, window_valid)
    trig_table = build_table(F, LAGS)
    norm_scale = 1.0 / math.sqrt(F * W)
    results = []
    for turn_index in range(TURNS):
        selected = jnp.take(whitened, sources[turn_index], axis=1)
        stacked = lax.map(lambda single: cross_block(single[:, None, :], whitened, trig_table)[0], jnp.moveaxis(selected, 1, 0))
        results.append(stacked * norm_scale)
    return jnp.stack(results, axis=0)
```

```python
import functools
import math

import jax
import jax.numpy as jnp
import ml_dtypes
import numpy as np
from jax import lax
from jax.experimental import pallas as pl
from jax.experimental.pallas import tpu as pltpu
from jax.sharding import PartitionSpec as P

LAGS = 256
LANES = 128
CHUNK = 256
MESH = pl.DeviceIdType.MESH


def build_table(freq_count, lag_count):
    shifts = np.arange(lag_count, dtype=np.int64) - lag_count // 2
    freq_bins = np.arange(freq_count, dtype=np.int64)
    phase_index = (freq_bins[:, None] * shifts[None, :]) % (2 * freq_count)
    angles = phase_index.astype(np.float32) * np.float32(math.pi / freq_count)
    table = np.stack([np.cos(angles), -np.sin(angles)]).astype(ml_dtypes.bfloat16)
    table = table.reshape(2, freq_count // CHUNK, CHUNK, lag_count).transpose(1, 0, 2, 3)
    return np.ascontiguousarray(table.reshape(freq_count // CHUNK, 2 * CHUNK, lag_count))


def kernel(
    chan_size, win_size, turns, spec_hbm, trig_hbm, valid_ref, sources_ref, out_ref,
    spec, trig, real, imag, gathered, srcs, sent, kept, received, acc,
    local_sem, gather_send, gather_recv, stack_send, stack_recv,
):
    chan_local = valid_ref.shape[1]
    rows = spec.shape[0] // chan_local
    me_c, me_w = lax.axis_index("chan"), lax.axis_index("win")
    share = chan_size // win_size
    wins_half = win_size // 2
    per_half = share * wins_half
    group = math.gcd(per_half, 4)

    spec_copy = pltpu.make_async_copy(spec_hbm, spec, local_sem.at[0])
    spec_copy.start()
    trig_copy = pltpu.make_async_copy(trig_hbm, trig, local_sem.at[1])
    trig_copy.start()
    barrier = pltpu.get_barrier_semaphore()
    for d in range(1, chan_size):
        pl.semaphore_signal(
            barrier, inc=1, device_id={"chan": lax.rem(me_c + d, chan_size)}, device_id_type=MESH
        )
    for d in range(1, win_size):
        pl.semaphore_signal(
            barrier, inc=1, device_id={"win": lax.rem(me_w + d, win_size)}, device_id_type=MESH
        )
    valid = valid_ref[...].astype(jnp.float32)
    lane = lax.broadcasted_iota(jnp.int32, (1, chan_local), 1)
    inverse = 1.0 / (rows * LANES)
    spec_copy.wait()

    for t in range(turns):
        row = jnp.full((1, LANES), sources_ref[t, me_c] - me_c * chan_local, jnp.int32)
        wanted = jnp.broadcast_to(row, (rows, LANES))
        picked = jnp.zeros((rows, LANES), jnp.float32)
        for c in range(chan_local):
            picked = jnp.where(wanted == c, spec[c * rows:(c + 1) * rows, :], picked)
        power = jnp.sum(jnp.sum(picked * picked, axis=0, keepdims=True), axis=1, keepdims=True)
        flag = jnp.sum(jnp.where(lane == row[:, :chan_local], valid, 0.0), axis=1, keepdims=True)
        scale = flag / jnp.sqrt(power * inverse + 1e-05)
        gathered[me_c, t * rows:(t + 1) * rows, :] = (picked * scale).astype(jnp.bfloat16)

    pl.semaphore_wait(barrier, chan_size - 1 + win_size - 1)

    def gather_copy(peer, owner):
        return pltpu.make_async_remote_copy(
            src_ref=gathered.at[owner],
            dst_ref=gathered.at[owner],
            send_sem=gather_send.at[peer],
            recv_sem=gather_recv.at[owner],
            device_id={"chan": peer},
            device_id_type=MESH,
        )

    for d in range(chan_size - 1, 0, -1):
        gather_copy(lax.rem(me_c + d, chan_size), me_c).start()

    squares = jnp.zeros((chan_local, LANES), jnp.float32)
    for i in range(rows):
        value = spec[pl.ds(i, chan_local, stride=rows), :]
        squares = squares + value * value
    power = jnp.sum(squares, axis=1, keepdims=True)
    across = lax.broadcasted_iota(jnp.int32, (chan_local, chan_local), 0)
    along = lax.broadcasted_iota(jnp.int32, (chan_local, chan_local), 1)
    flags = jnp.sum(jnp.where(across == along, valid, 0.0), axis=1, keepdims=True)
    scale = flags / jnp.sqrt(power * inverse + 1e-05)
    scale = jnp.broadcast_to(scale, (chan_local, LANES))
    for i in range(rows):
        value = spec[pl.ds(i, chan_local, stride=rows), :] * scale
        part = imag if i % 2 else real
        lanes = slice(i // 2 * LANES, i // 2 * LANES + LANES)
        part[:, lanes] = value.astype(jnp.bfloat16).astype(jnp.float32)
    trig_copy.wait()

    def stack_copy(target, origin):
        return pltpu.make_async_remote_copy(
            src_ref=sent.at[pl.ds(target * share, share)],
            dst_ref=received.at[origin],
            send_sem=stack_send.at[target],
            recv_sem=stack_recv.at[origin],
            device_id={"win": target},
            device_id_type=MESH,
        )

    my_half = me_w // wins_half
    for phase in range(2):
        half = my_half if phase else 1 - my_half
        first = half * per_half

        def arrive(i, carry, first=first):
            owner = first + i

            @pl.when(owner != me_c)
            def _():
                gather_copy(me_c, owner).wait_recv()

            srcs[owner] = gathered[owner].astype(jnp.float32)
            return carry

        lax.fori_loop(0, per_half, arrive, 0)

        def block(b, carry, first=first, phase=phase):
            slot = first + b * group
            acc[...] = jnp.zeros_like(acc)

            def step(k, inner):
                bins = pl.ds(pl.multiple_of(k * CHUNK, CHUNK), CHUNK)
                x, y = real[:, bins], imag[:, bins]
                reals, imags = [], []
                for i in range(group):
                    for t in range(turns):
                        base = t * rows + k * (2 * CHUNK // LANES)
                        pieces = [
                            srcs[slot + i, pl.ds(base + j, 1), :] for j in range(2 * CHUNK // LANES)
                        ]
                        a = jnp.concatenate(pieces[0::2], axis=1)
                        b_ = jnp.concatenate(pieces[1::2], axis=1)
                        reals.append((a * x + b_ * y).astype(jnp.bfloat16))
                        imags.append((b_ * x - a * y).astype(jnp.bfloat16))
                cross = jnp.concatenate(
                    [jnp.concatenate(reals, axis=0), jnp.concatenate(imags, axis=0)], axis=1
                )
                acc[...] += jnp.dot(cross, trig[k], preferred_element_type=jnp.float32)
                return inner

            lax.fori_loop(0, real.shape[1] // CHUNK, step, 0, unroll=2)
            for i in range(group):
                for t in range(turns):
                    at = (i * turns + t) * chan_local
                    value = acc[at:at + chan_local, :]
                    sent[slot + i, t] = value.astype(jnp.bfloat16)
                    if phase:
                        kept[b * group + i, t] = value
            return carry

        if per_half == group:
            block(0, 0)
        else:
            lax.fori_loop(0, per_half // group, block, 0)
        for i in range(wins_half):
            target = half * wins_half + i
            if phase == 0:
                stack_copy(target, me_w).start()
            else:

                @pl.when(target != me_w)
                def _(target=target):
                    stack_copy(target, me_w).start()

    base = lax.rem(me_w, wins_half) * share
    others = [lax.rem(me_w + d, win_size) for d in range(1, win_size)]
    for other in others:
        stack_copy(me_w, other).wait_recv()
    for j in range(share):
        for t in range(turns):
            total = kept[base + j, t]
            for other in others:
                total = total + received[other, j, t].astype(jnp.float32)
            out_ref[t, j] = total
    for d in range(1, chan_size):
        gather_copy(lax.rem(me_c + d, chan_size), me_c).wait_send()
    for other in others:
        stack_copy(other, me_w).wait_send()


def local(spectra, sources, window_valid):
    chan_size, win_size = lax.axis_size("chan"), lax.axis_size("win")
    win_local, chan_local, _, freq_count = spectra.shape
    turns, slots = sources.shape
    assert win_local == 1 and slots == chan_size and chan_size % win_size == 0
    blocks = freq_count // LANES
    rows = 2 * blocks
    share = slots // win_size
    per_half = slots // 2
    group = math.gcd(per_half, 4)
    spread = spectra.reshape(chan_local, 2, blocks, LANES).transpose(0, 2, 1, 3)
    spread = spread.reshape(chan_local * rows, LANES)
    table = jnp.asarray(build_table(freq_count, LAGS))
    norm_scale = 1.0 / math.sqrt(freq_count * win_local * win_size)
    stacked = pl.pallas_call(
        functools.partial(kernel, chan_size, win_size, turns),
        out_shape=jax.ShapeDtypeStruct((turns, share, chan_local, LAGS), jnp.float32),
        in_specs=[
            pl.BlockSpec(memory_space=pltpu.HBM),
            pl.BlockSpec(memory_space=pltpu.HBM),
            pl.BlockSpec(memory_space=pltpu.VMEM),
            pl.BlockSpec(memory_space=pltpu.SMEM),
        ],
        out_specs=pl.BlockSpec(memory_space=pltpu.VMEM),
        scratch_shapes=[
            pltpu.VMEM((chan_local * rows, LANES), jnp.float32),
            pltpu.VMEM(table.shape, jnp.bfloat16),
            pltpu.VMEM((chan_local, freq_count), jnp.float32),
            pltpu.VMEM((chan_local, freq_count), jnp.float32),
            pltpu.VMEM((slots, turns * rows, LANES), jnp.bfloat16),
            pltpu.VMEM((slots, turns * rows, LANES), jnp.float32),
            pltpu.VMEM((slots, turns, chan_local, LAGS), jnp.bfloat16),
            pltpu.VMEM((per_half, turns, chan_local, LAGS), jnp.float32),
            pltpu.VMEM((win_size, share, turns, chan_local, LAGS), jnp.bfloat16),
            pltpu.VMEM((group * turns * chan_local, LAGS), jnp.float32),
            pltpu.SemaphoreType.DMA((2,)),
            pltpu.SemaphoreType.DMA((chan_size,)),
            pltpu.SemaphoreType.DMA((chan_size,)),
            pltpu.SemaphoreType.DMA((win_size,)),
            pltpu.SemaphoreType.DMA((win_size,)),
        ],
        compiler_params=pltpu.CompilerParams(
            collective_id=0, has_side_effects=True, vmem_limit_bytes=63 * 1024 * 1024
        ),
        cost_estimate=pl.CostEstimate(
            flops=2 * turns * slots * chan_local * 2 * freq_count * LAGS,
            bytes_accessed=8 * 1024 * 1024,
            transcendentals=0,
        ),
    )(spread, table, window_valid, sources)
    return stacked * norm_scale


def solution(mesh):
    placed = (P("win", "chan", None, None), P(), P("win", "chan"))
    return jax.shard_map(
        local, mesh=mesh, in_specs=placed, out_specs=P(None, "win", "chan", None), check_vma=False
    )
```

```python
import functools
import math

import jax
import jax.numpy as jnp
import ml_dtypes
import numpy as np
from jax import lax
from jax.experimental import pallas as pl
from jax.experimental.pallas import tpu as pltpu
from jax.sharding import PartitionSpec as P

LAGS = 256
LANES = 128
CHUNK = 256
MESH = pl.DeviceIdType.MESH


def build_table(freq_count, lag_count):
    shifts = np.arange(lag_count, dtype=np.int64) - lag_count // 2
    freq_bins = np.arange(freq_count, dtype=np.int64)
    phase_index = (freq_bins[:, None] * shifts[None, :]) % (2 * freq_count)
    angles = phase_index.astype(np.float32) * np.float32(math.pi / freq_count)
    table = np.stack([np.cos(angles), -np.sin(angles)]).astype(ml_dtypes.bfloat16)
    table = table.reshape(2, freq_count // CHUNK, CHUNK, lag_count).transpose(1, 0, 2, 3)
    return np.ascontiguousarray(table.reshape(freq_count // CHUNK, 2 * CHUNK, lag_count))


def kernel(
    chan_size, win_size, turns, spec_hbm, trig_hbm, valid_hbm, sources_hbm, out_ref,
    spec, trig, valid_ref, sources_ref, real, imag, gathered, srcs, sent, kept, received, acc,
    local_sem, gather_send, gather_recv, stack_send, stack_recv,
):
    chan_local = valid_ref.shape[1]
    rows = spec.shape[0] // chan_local
    me_c, me_w = lax.axis_index("chan"), lax.axis_index("win")
    share = chan_size // win_size
    wins_half = win_size // 2
    per_half = share * wins_half
    group = math.gcd(per_half, 4)

    barrier = pltpu.get_barrier_semaphore()
    for d in range(1, win_size):
        pl.semaphore_signal(
            barrier, inc=1, device_id={"win": lax.rem(me_w + d, win_size)}, device_id_type=MESH
        )
    for d in range(1, chan_size):
        pl.semaphore_signal(
            barrier, inc=1, device_id={"chan": lax.rem(me_c + d, chan_size)}, device_id_type=MESH
        )
    sources_copy = pltpu.make_async_copy(sources_hbm, sources_ref, local_sem.at[2])
    sources_copy.start()
    valid_copy = pltpu.make_async_copy(valid_hbm, valid_ref, local_sem.at[3])
    valid_copy.start()
    spec_copy = pltpu.make_async_copy(spec_hbm, spec, local_sem.at[0])
    spec_copy.start()
    trig_copy = pltpu.make_async_copy(trig_hbm, trig, local_sem.at[1])
    trig_copy.start()
    sources_copy.wait()
    valid_copy.wait()
    valid = valid_ref[...].astype(jnp.float32)
    lane = lax.broadcasted_iota(jnp.int32, (1, chan_local), 1)
    inverse = 1.0 / (rows * LANES)
    spec_copy.wait()

    for t in range(turns):
        row = jnp.full((1, LANES), sources_ref[t, me_c] - me_c * chan_local, jnp.int32)
        wanted = jnp.broadcast_to(row, (rows, LANES))
        picked = jnp.zeros((rows, LANES), jnp.float32)
        for c in range(chan_local):
            picked = jnp.where(wanted == c, spec[c * rows:(c + 1) * rows, :], picked)
        power = jnp.sum(jnp.sum(picked * picked, axis=0, keepdims=True), axis=1, keepdims=True)
        flag = jnp.sum(jnp.where(lane == row[:, :chan_local], valid, 0.0), axis=1, keepdims=True)
        scale = flag / jnp.sqrt(power * inverse + 1e-05)
        gathered[me_c, t * rows:(t + 1) * rows, :] = (picked * scale).astype(jnp.bfloat16)

    pl.semaphore_wait(barrier, chan_size - 1 + win_size - 1)

    def gather_copy(peer, owner):
        return pltpu.make_async_remote_copy(
            src_ref=gathered.at[owner],
            dst_ref=gathered.at[owner],
            send_sem=gather_send.at[peer],
            recv_sem=gather_recv.at[owner],
            device_id={"chan": peer},
            device_id_type=MESH,
        )

    for d in range(chan_size - 1, 0, -1):
        gather_copy(lax.rem(me_c + d, chan_size), me_c).start()

    squares = jnp.zeros((chan_local, LANES), jnp.float32)
    for i in range(rows):
        value = spec[pl.ds(i, chan_local, stride=rows), :]
        squares = squares + value * value
    power = jnp.sum(squares, axis=1, keepdims=True)
    across = lax.broadcasted_iota(jnp.int32, (chan_local, chan_local), 0)
    along = lax.broadcasted_iota(jnp.int32, (chan_local, chan_local), 1)
    flags = jnp.sum(jnp.where(across == along, valid, 0.0), axis=1, keepdims=True)
    scale = flags / jnp.sqrt(power * inverse + 1e-05)
    scale = jnp.broadcast_to(scale, (chan_local, LANES))
    for i in range(rows):
        value = spec[pl.ds(i, chan_local, stride=rows), :] * scale
        part = imag if i % 2 else real
        lanes = slice(i // 2 * LANES, i // 2 * LANES + LANES)
        part[:, lanes] = value.astype(jnp.bfloat16).astype(jnp.float32)
    trig_copy.wait()

    def stack_copy(target, origin):
        return pltpu.make_async_remote_copy(
            src_ref=sent.at[pl.ds(target * share, share)],
            dst_ref=received.at[origin],
            send_sem=stack_send.at[target],
            recv_sem=stack_recv.at[origin],
            device_id={"win": target},
            device_id_type=MESH,
        )

    my_half = me_w // wins_half
    for phase in range(2):
        half = my_half if phase else 1 - my_half
        first = half * per_half

        def arrive(i, carry, first=first):
            owner = first + i

            @pl.when(owner != me_c)
            def _():
                gather_copy(me_c, owner).wait_recv()

            srcs[owner] = gathered[owner].astype(jnp.float32)
            return carry

        lax.fori_loop(0, per_half, arrive, 0)

        def block(b, carry, first=first, phase=phase):
            slot = first + b * group
            acc[...] = jnp.zeros_like(acc)

            def step(k, inner):
                bins = pl.ds(pl.multiple_of(k * CHUNK, CHUNK), CHUNK)
                x, y = real[:, bins], imag[:, bins]
                reals, imags = [], []
                for i in range(group):
                    for t in range(turns):
                        base = t * rows + k * (2 * CHUNK // LANES)
                        pieces = [
                            srcs[slot + i, pl.ds(base + j, 1), :] for j in range(2 * CHUNK // LANES)
                        ]
                        a = jnp.concatenate(pieces[0::2], axis=1)
                        b_ = jnp.concatenate(pieces[1::2], axis=1)
                        reals.append((a * x + b_ * y).astype(jnp.bfloat16))
                        imags.append((b_ * x - a * y).astype(jnp.bfloat16))
                cross = jnp.concatenate(
                    [jnp.concatenate(reals, axis=0), jnp.concatenate(imags, axis=0)], axis=1
                )
                acc[...] += jnp.dot(cross, trig[k], preferred_element_type=jnp.float32)
                return inner

            lax.fori_loop(0, real.shape[1] // CHUNK, step, 0, unroll=8)
            for i in range(group):
                for t in range(turns):
                    at = (i * turns + t) * chan_local
                    value = acc[at:at + chan_local, :]
                    sent[slot + i, t] = value.astype(jnp.bfloat16)
                    if phase:
                        kept[b * group + i, t] = value
            return carry

        if per_half == group:
            block(0, 0)
        else:
            lax.fori_loop(0, per_half // group, block, 0)
        for i in range(wins_half):
            target = half * wins_half + i
            if phase == 0:
                stack_copy(target, me_w).start()
            else:

                @pl.when(target != me_w)
                def _(target=target):
                    stack_copy(target, me_w).start()

    base = lax.rem(me_w, wins_half) * share
    others = [lax.rem(me_w + d, win_size) for d in range(1, win_size)]
    for other in others:
        stack_copy(me_w, other).wait_recv()
    for j in range(share):
        for t in range(turns):
            total = kept[base + j, t]
            for other in others:
                total = total + received[other, j, t].astype(jnp.float32)
            out_ref[t, j] = total
    for d in range(1, chan_size):
        gather_copy(lax.rem(me_c + d, chan_size), me_c).wait_send()
    for other in others:
        stack_copy(other, me_w).wait_send()


def local(spectra, sources, window_valid):
    chan_size, win_size = lax.axis_size("chan"), lax.axis_size("win")
    win_local, chan_local, _, freq_count = spectra.shape
    turns, slots = sources.shape
    assert win_local == 1 and slots == chan_size and chan_size % win_size == 0
    blocks = freq_count // LANES
    rows = 2 * blocks
    share = slots // win_size
    per_half = slots // 2
    group = math.gcd(per_half, 4)
    spread = spectra.reshape(chan_local, 2, blocks, LANES).transpose(0, 2, 1, 3)
    spread = spread.reshape(chan_local * rows, LANES)
    table = jnp.asarray(build_table(freq_count, LAGS))
    norm_scale = 1.0 / math.sqrt(freq_count * win_local * win_size)
    stacked = pl.pallas_call(
        functools.partial(kernel, chan_size, win_size, turns),
        out_shape=jax.ShapeDtypeStruct((turns, share, chan_local, LAGS), jnp.float32),
        in_specs=[
            pl.BlockSpec(memory_space=pltpu.HBM),
            pl.BlockSpec(memory_space=pltpu.HBM),
            pl.BlockSpec(memory_space=pltpu.HBM),
            pl.BlockSpec(memory_space=pltpu.HBM),
        ],
        out_specs=pl.BlockSpec(memory_space=pltpu.VMEM),
        scratch_shapes=[
            pltpu.VMEM((chan_local * rows, LANES), jnp.float32),
            pltpu.VMEM(table.shape, jnp.bfloat16),
            pltpu.VMEM(window_valid.shape, jnp.int32),
            pltpu.SMEM(sources.shape, jnp.int32),
            pltpu.VMEM((chan_local, freq_count), jnp.float32),
            pltpu.VMEM((chan_local, freq_count), jnp.float32),
            pltpu.VMEM((slots, turns * rows, LANES), jnp.bfloat16),
            pltpu.VMEM((slots, turns * rows, LANES), jnp.float32),
            pltpu.VMEM((slots, turns, chan_local, LAGS), jnp.bfloat16),
            pltpu.VMEM((per_half, turns, chan_local, LAGS), jnp.float32),
            pltpu.VMEM((win_size, share, turns, chan_local, LAGS), jnp.bfloat16),
            pltpu.VMEM((group * turns * chan_local, LAGS), jnp.float32),
            pltpu.SemaphoreType.DMA((4,)),
            pltpu.SemaphoreType.DMA((chan_size,)),
            pltpu.SemaphoreType.DMA((chan_size,)),
            pltpu.SemaphoreType.DMA((win_size,)),
            pltpu.SemaphoreType.DMA((win_size,)),
        ],
        compiler_params=pltpu.CompilerParams(
            collective_id=0, has_side_effects=True, vmem_limit_bytes=63 * 1024 * 1024
        ),
        cost_estimate=pl.CostEstimate(
            flops=2 * turns * slots * chan_local * 2 * freq_count * LAGS,
            bytes_accessed=8 * 1024 * 1024,
            transcendentals=0,
        ),
    )(spread, table, window_valid, sources)
    return stacked * norm_scale


def solution(mesh):
    placed = (P("win", "chan", None, None), P(), P("win", "chan"))
    return jax.shard_map(
        local, mesh=mesh, in_specs=placed, out_specs=P(None, "win", "chan", None), check_vma=False
    )
```

```python
import functools
import math

import jax
import jax.numpy as jnp
import ml_dtypes
import numpy as np
from jax import lax
from jax.experimental import pallas as pl
from jax.experimental.pallas import tpu as pltpu
from jax.sharding import PartitionSpec as P

LAGS = 256
LANES = 128
CHUNK = 256
MESH = pl.DeviceIdType.MESH


def build_table(freq_count, lag_count):
    shifts = np.arange(lag_count, dtype=np.int64) - lag_count // 2
    freq_bins = np.arange(freq_count, dtype=np.int64)
    phase_index = (freq_bins[:, None] * shifts[None, :]) % (2 * freq_count)
    angles = phase_index.astype(np.float32) * np.float32(math.pi / freq_count)
    table = np.stack([np.cos(angles), -np.sin(angles)]).astype(ml_dtypes.bfloat16)
    table = table.reshape(2, freq_count // CHUNK, CHUNK, lag_count).transpose(1, 0, 2, 3)
    return np.ascontiguousarray(table.reshape(freq_count // CHUNK, 2 * CHUNK, lag_count))


def kernel(
    chan_size, win_size, turns, spec_hbm, trig_hbm, valid_hbm, sources_hbm, out_ref,
    spec, trig, valid_ref, sources_ref, real, imag, gathered, srcs, sent, kept, received, acc,
    local_sem, gather_send, gather_recv, stack_send, stack_recv,
):
    chan_local = valid_ref.shape[1]
    rows = spec.shape[0] // chan_local
    me_c, me_w = lax.axis_index("chan"), lax.axis_index("win")
    share = chan_size // win_size
    wins_half = win_size // 2
    group = math.gcd(share, 4)

    barrier = pltpu.get_barrier_semaphore()
    for d in range(1, win_size):
        pl.semaphore_signal(
            barrier, inc=1, device_id={"win": lax.rem(me_w + d, win_size)}, device_id_type=MESH
        )
    for d in range(1, chan_size):
        pl.semaphore_signal(
            barrier, inc=1, device_id={"chan": lax.rem(me_c + d, chan_size)}, device_id_type=MESH
        )
    sources_copy = pltpu.make_async_copy(sources_hbm, sources_ref, local_sem.at[2])
    sources_copy.start()
    valid_copy = pltpu.make_async_copy(valid_hbm, valid_ref, local_sem.at[3])
    valid_copy.start()
    spec_copy = pltpu.make_async_copy(spec_hbm, spec, local_sem.at[0])
    spec_copy.start()
    trig_copy = pltpu.make_async_copy(trig_hbm, trig, local_sem.at[1])
    trig_copy.start()
    sources_copy.wait()
    valid_copy.wait()
    valid = valid_ref[...].astype(jnp.float32)
    lane = lax.broadcasted_iota(jnp.int32, (1, chan_local), 1)
    inverse = 1.0 / (rows * LANES)
    spec_copy.wait()

    for t in range(turns):
        row = jnp.full((1, LANES), sources_ref[t, me_c] - me_c * chan_local, jnp.int32)
        wanted = jnp.broadcast_to(row, (rows, LANES))
        picked = jnp.zeros((rows, LANES), jnp.float32)
        for c in range(chan_local):
            picked = jnp.where(wanted == c, spec[c * rows:(c + 1) * rows, :], picked)
        power = jnp.sum(jnp.sum(picked * picked, axis=0, keepdims=True), axis=1, keepdims=True)
        flag = jnp.sum(jnp.where(lane == row[:, :chan_local], valid, 0.0), axis=1, keepdims=True)
        scale = flag / jnp.sqrt(power * inverse + 1e-05)
        gathered[me_c, t * rows:(t + 1) * rows, :] = (picked * scale).astype(jnp.bfloat16)

    pl.semaphore_wait(barrier, chan_size - 1 + win_size - 1)

    def gather_copy(peer, owner):
        return pltpu.make_async_remote_copy(
            src_ref=gathered.at[owner],
            dst_ref=gathered.at[owner],
            send_sem=gather_send.at[peer],
            recv_sem=gather_recv.at[owner],
            device_id={"chan": peer},
            device_id_type=MESH,
        )

    for d in range(chan_size - 1, 0, -1):
        gather_copy(lax.rem(me_c + d, chan_size), me_c).start()

    squares = jnp.zeros((chan_local, LANES), jnp.float32)
    for i in range(rows):
        value = spec[pl.ds(i, chan_local, stride=rows), :]
        squares = squares + value * value
    power = jnp.sum(squares, axis=1, keepdims=True)
    across = lax.broadcasted_iota(jnp.int32, (chan_local, chan_local), 0)
    along = lax.broadcasted_iota(jnp.int32, (chan_local, chan_local), 1)
    flags = jnp.sum(jnp.where(across == along, valid, 0.0), axis=1, keepdims=True)
    scale = flags / jnp.sqrt(power * inverse + 1e-05)
    scale = jnp.broadcast_to(scale, (chan_local, LANES))
    for i in range(rows):
        value = spec[pl.ds(i, chan_local, stride=rows), :] * scale
        part = imag if i % 2 else real
        lanes = slice(i // 2 * LANES, i // 2 * LANES + LANES)
        part[:, lanes] = value.astype(jnp.bfloat16).astype(jnp.float32)
    trig_copy.wait()

    def stack_copy(target, origin):
        return pltpu.make_async_remote_copy(
            src_ref=sent.at[pl.ds(target * share, share)],
            dst_ref=received.at[origin],
            send_sem=stack_send.at[target],
            recv_sem=stack_recv.at[origin],
            device_id={"win": target},
            device_id_type=MESH,
        )

    my_half = me_w // wins_half
    targets = [
        (1 - my_half) * wins_half + lax.rem(me_w + i, wins_half) for i in range(wins_half)
    ] + [my_half * wins_half + lax.rem(me_w + 1 + i, wins_half) for i in range(wins_half)]
    for target in targets:
        mine = target is targets[-1]
        first = target * share

        def arrive(i, carry, first=first):
            owner = first + i

            @pl.when(owner != me_c)
            def _():
                gather_copy(me_c, owner).wait_recv()

            srcs[owner] = gathered[owner].astype(jnp.float32)
            return carry

        lax.fori_loop(0, share, arrive, 0)

        def block(b, carry, first=first, mine=mine):
            slot = first + b * group
            acc[...] = jnp.zeros_like(acc)

            def step(k, inner):
                bins = pl.ds(pl.multiple_of(k * CHUNK, CHUNK), CHUNK)
                x, y = real[:, bins], imag[:, bins]
                reals, imags = [], []
                for i in range(group):
                    for t in range(turns):
                        base = t * rows + k * (2 * CHUNK // LANES)
                        pieces = [
                            srcs[slot + i, pl.ds(base + j, 1), :] for j in range(2 * CHUNK // LANES)
                        ]
                        a = jnp.concatenate(pieces[0::2], axis=1)
                        b_ = jnp.concatenate(pieces[1::2], axis=1)
                        reals.append((a * x + b_ * y).astype(jnp.bfloat16))
                        imags.append((b_ * x - a * y).astype(jnp.bfloat16))
                cross = jnp.concatenate(
                    [jnp.concatenate(reals, axis=0), jnp.concatenate(imags, axis=0)], axis=1
                )
                acc[...] += jnp.dot(cross, trig[k], preferred_element_type=jnp.float32)
                return inner

            lax.fori_loop(0, real.shape[1] // CHUNK, step, 0, unroll=8)
            for i in range(group):
                for t in range(turns):
                    at = (i * turns + t) * chan_local
                    value = acc[at:at + chan_local, :]
                    if mine:
                        kept[b * group + i, t] = value
                    else:
                        sent[slot + i, t] = value.astype(jnp.bfloat16)
            return carry

        if share == group:
            block(0, 0)
        else:
            lax.fori_loop(0, share // group, block, 0)
        if not mine:
            stack_copy(target, me_w).start()

    others = [lax.rem(me_w + d, win_size) for d in range(1, win_size)]
    for other in others:
        stack_copy(me_w, other).wait_recv()
    for j in range(share):
        for t in range(turns):
            total = kept[j, t]
            for other in others:
                total = total + received[other, j, t].astype(jnp.float32)
            out_ref[t, j] = total
    for d in range(1, chan_size):
        gather_copy(lax.rem(me_c + d, chan_size), me_c).wait_send()
    for other in others:
        stack_copy(other, me_w).wait_send()


def local(spectra, sources, window_valid):
    chan_size, win_size = lax.axis_size("chan"), lax.axis_size("win")
    win_local, chan_local, _, freq_count = spectra.shape
    turns, slots = sources.shape
    assert win_local == 1 and slots == chan_size and chan_size % win_size == 0
    blocks = freq_count // LANES
    rows = 2 * blocks
    share = slots // win_size
    group = math.gcd(share, 4)
    spread = spectra.reshape(chan_local, 2, blocks, LANES).transpose(0, 2, 1, 3)
    spread = spread.reshape(chan_local * rows, LANES)
    table = jnp.asarray(build_table(freq_count, LAGS))
    norm_scale = 1.0 / math.sqrt(freq_count * win_local * win_size)
    stacked = pl.pallas_call(
        functools.partial(kernel, chan_size, win_size, turns),
        out_shape=jax.ShapeDtypeStruct((turns, share, chan_local, LAGS), jnp.float32),
        in_specs=[
            pl.BlockSpec(memory_space=pltpu.HBM),
            pl.BlockSpec(memory_space=pltpu.HBM),
            pl.BlockSpec(memory_space=pltpu.HBM),
            pl.BlockSpec(memory_space=pltpu.HBM),
        ],
        out_specs=pl.BlockSpec(memory_space=pltpu.VMEM),
        scratch_shapes=[
            pltpu.VMEM((chan_local * rows, LANES), jnp.float32),
            pltpu.VMEM(table.shape, jnp.bfloat16),
            pltpu.VMEM(window_valid.shape, jnp.int32),
            pltpu.SMEM(sources.shape, jnp.int32),
            pltpu.VMEM((chan_local, freq_count), jnp.float32),
            pltpu.VMEM((chan_local, freq_count), jnp.float32),
            pltpu.VMEM((slots, turns * rows, LANES), jnp.bfloat16),
            pltpu.VMEM((slots, turns * rows, LANES), jnp.float32),
            pltpu.VMEM((slots, turns, chan_local, LAGS), jnp.bfloat16),
            pltpu.VMEM((share, turns, chan_local, LAGS), jnp.float32),
            pltpu.VMEM((win_size, share, turns, chan_local, LAGS), jnp.bfloat16),
            pltpu.VMEM((group * turns * chan_local, LAGS), jnp.float32),
            pltpu.SemaphoreType.DMA((4,)),
            pltpu.SemaphoreType.DMA((chan_size,)),
            pltpu.SemaphoreType.DMA((chan_size,)),
            pltpu.SemaphoreType.DMA((win_size,)),
            pltpu.SemaphoreType.DMA((win_size,)),
        ],
        compiler_params=pltpu.CompilerParams(
            collective_id=0, has_side_effects=True, vmem_limit_bytes=63 * 1024 * 1024
        ),
        cost_estimate=pl.CostEstimate(
            flops=2 * turns * slots * chan_local * 2 * freq_count * LAGS,
            bytes_accessed=8 * 1024 * 1024,
            transcendentals=0,
        ),
    )(spread, table, window_valid, sources)
    return stacked * norm_scale


def solution(mesh):
    placed = (P("win", "chan", None, None), P(), P("win", "chan"))
    return jax.shard_map(
        local, mesh=mesh, in_specs=placed, out_specs=P(None, "win", "chan", None), check_vma=False
    )
```
